128 devices in a mesh: seq: 8 (over y, core), pool: 16 (over x, z).
Axes of the slice: x: 4, y: 4, z: 4, core: 2. Of those that a mesh axis runs over, the one named last changes fastest.
Arguments:
- queries: bfloat16 [16, 4096, 4096], P('pool', 'seq'), may hold values from -6.5 to 6.5
- text_kv: bfloat16 [16, 4096, 1024], P('pool', 'seq'), may hold values from -6 to 6
- tile_embeds: bfloat16 [8, 2048, 8192], P('seq', 'pool'), may hold values from -400 to 400
- stored_kv: bfloat16 [8, 4096, 1024], P('seq', 'pool'), may hold values from -6 to 6
- w_kv: bfloat16 [8192, 1024], P('pool'), may hold values from -0.0625 to 0.0625
- block_source: int32 [16, 128], P(None, 'seq'), may hold values from 0 to 192, as said below
- block_mask: int32 [16, 128, 128], P('pool'), may hold values 0 or 1
Outputs:
- attended: bfloat16 [16, 4096, 4096], P('pool', 'seq')
The draws below stay inside these ranges and needn't reach their ends.
Inputs may be any that keep to these rules, and one draw needn't show every extreme that they name: `block_source`: 0 marks a text block; c > 0 names an entry of a device that holds the same sequence shard, as in the reference program. At most 2 blocks of one sequence shard of one request come from one device, and some shard reaches that in every draw. Each miss tile is named at most once; a cached block may be named by several requests.
All inputs are finite; a program needn't handle non-finite values. No bound on the sum of `block_mask` on one device may be relied on, other than what follows from the above.
Results may differ from the reference program's by a relative error of at most 0.013.
Values may be sent and summed in bfloat16 or wider, within the bound.
No kernel may reach another device: no remote copies, remote signals or barrier semaphores. Data moves between devices by JAX's collectives and lax.ppermute only.
A program may use at most 192 MiB of HBM per device.

```python
import math
from functools import partial
import jax
import jax.numpy as jnp
from jax import lax

MODEL_WIDTH = 8192
QUERY_HEADS = 32
KEY_HEADS = 4
HEAD_SIZE = 128
BLOCK_ROWS = 32
SOURCE_CAP = 2
SHARD_BLOCKS = 16
STORE_SLOTS = 8
MISS_TILES = 4
KV_WIDTH = 512
SHARD_TOKENS = 512
SEQ_BLOCKS = 128
SEQUENCE = 4096
REQUESTS = 16
N_SEQ = 8
N_POOL = 16


def draw_queries(key, part):
    key = jax.random.fold_in(key, 21)
    shape = (REQUESTS, SEQUENCE, QUERY_HEADS * HEAD_SIZE)
    values = jnp.clip(jax.random.normal(key, shape, jnp.float32), -6.0, 6.0)
    return values.astype(jnp.bfloat16)


def draw_text_kv(key, part):
    key = jax.random.fold_in(key, 22)
    shape = (REQUESTS, SEQUENCE, 2 * KV_WIDTH)
    values = jnp.clip(jax.random.normal(key, shape, jnp.float32), -6.0, 6.0)
    return values.astype(jnp.bfloat16)


def draw_tile_embeds(key, part):
    key = jax.random.fold_in(key, 23)
    row_count = N_POOL * MISS_TILES * BLOCK_ROWS
    shape = (N_SEQ, row_count, MODEL_WIDTH)
    column_scale = jnp.exp(jax.random.uniform(jax.random.fold_in(key, 2), (1, 1, MODEL_WIDTH), jnp.float32, 0.0, math.log(10.0)))
    base = jnp.clip(jax.random.normal(jax.random.fold_in(key, 3), shape, jnp.float32), -4.0, 4.0)
    row_scale = jnp.exp(jax.random.uniform(jax.random.fold_in(key, 1), (N_SEQ, row_count, 1), jnp.float32, 0.0, math.log(10.0)))
    return (base * row_scale * column_scale).astype(jnp.bfloat16)


def draw_block_source(key, part):
    key = jax.random.fold_in(key, 11)
    pair_count = SHARD_BLOCKS // SOURCE_CAP
    entries = STORE_SLOTS + MISS_TILES
    shape = (REQUESTS, N_SEQ, N_POOL)
    heat = jax.random.randint(jax.random.fold_in(key, 1), (1, N_SEQ, N_POOL), 0, 4)
    noise = jax.random.randint(jax.random.fold_in(key, 2), shape, 0, 4096)
    scores = (noise + heat * 4096) * N_POOL + lax.broadcasted_iota(jnp.int32, shape, 2)
    chosen = lax.top_k(scores, pair_count)[1].astype(jnp.int32)
    block_ids = lax.iota(jnp.int32, SHARD_BLOCKS)
    pair_of = block_ids // SOURCE_CAP
    within = block_ids % SOURCE_CAP
    pool_of = jnp.take(chosen, pair_of, axis=2)
    blocks_shape = (REQUESTS, N_SEQ, SHARD_BLOCKS)
    coin = jax.random.randint(jax.random.fold_in(key, 3), blocks_shape, 0, 5)
    is_image = (within == 0)[None, None, :] | (pair_of == 0)[None, None, :] | (coin < 4)
    request_ids = lax.broadcasted_iota(jnp.int32, blocks_shape, 0)
    tile_ids = (request_ids - pool_of - 1) % N_POOL
    is_miss = (within == 0)[None, None, :] & (tile_ids < MISS_TILES)
    slot_ids = jax.random.randint(jax.random.fold_in(key, 4), blocks_shape, 0, STORE_SLOTS)
    entry_ids = jnp.where(is_miss, STORE_SLOTS + tile_ids, slot_ids)
    codes = jnp.where(is_image, pool_of * entries + entry_ids + 1, 0)
    return codes.reshape(REQUESTS, N_SEQ * SHARD_BLOCKS).astype(jnp.int32)


def touch_ends(values, rng, smallest, largest):
    dims = values.shape
    index_at = [jax.random.randint(jax.random.fold_in(rng, axis), (), 0, dims[axis]) for axis in range(len(dims))]
    values = values.at[tuple(index_at)].set(smallest)
    longest = dims.index(max(dims))
    index_at[longest] = (index_at[longest] + 1) % dims[longest]
    return values.at[tuple(index_at)].set(largest)


def levels(key, shape, cuts, smallest, high):
    loudness = 1.0
    for dim, blocks in cuts:
        steps = jax.random.uniform(jax.random.fold_in(jax.random.fold_in(key, 6), dim), (blocks,), jnp.float32, smallest / len(cuts), high / len(cuts))
        loudness = loudness * jnp.repeat(jnp.exp(steps), shape[dim] // blocks).reshape((-1,) + (1,) * (len(shape) - 1 - dim))
    return loudness


def gaussian(rng, dims, spread, most, split=(), kind=jnp.bfloat16):
    values = jax.random.normal(rng, dims, jnp.float32) * spread
    if len(split) > 0:
        values = levels(rng, dims, split, -0.22, 0.18) * values
    return jnp.clip(values, min=-most, max=most).astype(kind)


def setup_inputs(seed: int = 0) -> dict:
    splits = jax.random.split(jax.random.key(seed), 8)
    return {
        "queries": draw_queries(jax.random.fold_in(splits[7], 71), 0),
        "text_kv": draw_text_kv(jax.random.fold_in(splits[7], 71), 0),
        "tile_embeds": draw_tile_embeds(jax.random.fold_in(splits[7], 71), 0),
        "stored_kv": gaussian(splits[3], (N_SEQ, N_POOL * STORE_SLOTS * BLOCK_ROWS, 2 * KV_WIDTH), 1.0, 6.0, ((0, 8), (1, 16))),
        "w_kv": gaussian(splits[4], (MODEL_WIDTH, 2 * KV_WIDTH), MODEL_WIDTH ** -0.5, 0.0625, ((0, 16),)),
        "block_source": draw_block_source(jax.random.fold_in(splits[7], 71), 0),
        "block_mask": touch_ends((jax.random.randint(splits[6], (REQUESTS, SEQ_BLOCKS, SEQ_BLOCKS), 0, 4) < 3).astype(jnp.int32), jax.random.fold_in(splits[6], 1), 0, 1),
    }


big_negative = -1e+30
eps_norm = 1e-06

def encode_row(tile_block, w_kv):
    tiles_f32 = tile_block.astype(jnp.float32)
    mean_square = lax.optimization_barrier(jnp.mean(tiles_f32 * tiles_f32, axis=-1, keepdims=True))
    normed = (tiles_f32 * lax.rsqrt(mean_square + eps_norm)).astype(jnp.bfloat16)
    return jnp.dot(normed, w_kv, preferred_element_type=jnp.float32).astype(jnp.bfloat16)

def attend_request(request_data):
    query_rows, kv_rows, mask_table = request_data
    kv_width = KEY_HEADS * HEAD_SIZE
    group_size = QUERY_HEADS // KEY_HEADS
    key_rows = kv_rows[:, :kv_width].reshape(SEQUENCE, KEY_HEADS, HEAD_SIZE).astype(jnp.float32)
    value_rows = kv_rows[:, kv_width:].reshape(SEQUENCE, KEY_HEADS, HEAD_SIZE).astype(jnp.float32)
    key_pos = jnp.arange(SEQUENCE).astype(jnp.int32)
    key_block = key_pos // BLOCK_ROWS
    shaped = query_rows.reshape(N_SEQ, SHARD_TOKENS, KEY_HEADS, group_size, HEAD_SIZE)

    def attend_block(block_data):
        block_queries, shard_index = block_data
        positions = shard_index * SHARD_TOKENS + jnp.arange(SHARD_TOKENS).astype(jnp.int32)
        query_block = positions // BLOCK_ROWS
        mask_rows = mask_table[query_block][:, key_block]
        allowed = (key_pos[None, :] <= positions[:, None]) & ((key_block[None, :] == query_block[:, None]) | (mask_rows == 1))
        scores = jnp.einsum('qhgd,khd->hgqk', block_queries.astype(jnp.float32), key_rows) * HEAD_SIZE ** (-0.5)
        scores = jnp.where(allowed, scores, big_negative)
        row_max = lax.optimization_barrier(jnp.max(scores, axis=-1, keepdims=True))
        weights = jnp.where(allowed, jnp.exp(scores - row_max), 0.0)
        denominator = lax.optimization_barrier(jnp.sum(weights, axis=-1))
        rounded = lax.optimization_barrier(weights.astype(jnp.bfloat16)).astype(jnp.float32)
        summed = jnp.einsum('hgqk,khd->hgqd', rounded, value_rows)
        result = summed / denominator[..., None]
        return jnp.transpose(result, (2, 0, 1, 3)).reshape(SHARD_TOKENS, QUERY_HEADS * HEAD_SIZE).astype(jnp.bfloat16)
    shard_ids = jnp.arange(N_SEQ).astype(jnp.int32)
    return lax.map(attend_block, (shaped, shard_ids)).reshape(SEQUENCE, QUERY_HEADS * HEAD_SIZE)

def reference(queries, text_kv, tile_embeds, stored_kv, w_kv, block_source, block_mask):
    channels = 2 * KEY_HEADS * HEAD_SIZE
    entries = STORE_SLOTS + MISS_TILES
    encoded = lax.map(partial(encode_row, w_kv=w_kv), tile_embeds)
    encoded = encoded.reshape(N_SEQ, N_POOL, MISS_TILES, BLOCK_ROWS, channels)
    stored = stored_kv.reshape(N_SEQ, N_POOL, STORE_SLOTS, BLOCK_ROWS, channels)
    block_table = jnp.concatenate([stored, encoded], axis=2).reshape(N_SEQ, N_POOL * entries, BLOCK_ROWS, channels)
    shard_of_block = (jnp.arange(SEQ_BLOCKS) // SHARD_BLOCKS).astype(jnp.int32)
    source_index = jnp.maximum(block_source - 1, 0).astype(jnp.int32)
    fetched = block_table[shard_of_block[None, :], source_index]
    text_blocks = text_kv.reshape(REQUESTS, SEQ_BLOCKS, BLOCK_ROWS, channels)
    kv_all = jnp.where((block_source > 0)[:, :, None, None], fetched, text_blocks).reshape(REQUESTS, SEQUENCE, channels)
    return lax.map(attend_request, (queries, kv_all, block_mask))
```

```python
import functools
import jax
import jax.numpy as jnp
from jax import lax
from jax.experimental import pallas as pl
from jax.experimental.pallas import tpu as pltpu
from jax.sharding import PartitionSpec as P

HEAD_SIZE = 128
BLOCK_ROWS = 32
SOURCE_CAP = 2
CHUNK = 512
KEY_TILE = 1024
SEQ_BLOCKS = 128
NEGATIVE = -1e30
EPS_NORM = 1e-06
LOG2_SCALE = HEAD_SIZE**-0.5 * 1.4426950408889634

bf16 = jnp.bfloat16
f32 = jnp.float32


def matmul(a, b):
    return lax.dot_general(a, b, (((1,), (0,)), ((), ())), preferred_element_type=f32)


def iota(shape, dim):
    return lax.broadcasted_iota(jnp.int32, shape, dim)


def build_keys(k_ref, v_ref, mask_ref, keys, values):
    square = (SEQ_BLOCKS, SEQ_BLOCKS)
    query_block, key_block = iota(square, 0), iota(square, 1)
    allowed = ((mask_ref[...] == 1) & (key_block < query_block)) | (key_block == query_block)
    bias = jnp.where(allowed, 0.0, NEGATIVE).astype(bf16)
    per_chunk = CHUNK // BLOCK_ROWS
    for t in range(k_ref.shape[0] // CHUNK):
        rows = slice(t * CHUNK, (t + 1) * CHUNK)
        spread = iota((SEQ_BLOCKS, CHUNK), 1) // BLOCK_ROWS + t * per_chunk
        spread = (spread == iota((SEQ_BLOCKS, CHUNK), 0)).astype(bf16)
        keys[0:HEAD_SIZE, rows] = k_ref[rows, :].T
        keys[HEAD_SIZE:, rows] = matmul(bias, spread).astype(bf16)
        values[rows, 0:HEAD_SIZE] = v_ref[rows, :]
        values[rows, HEAD_SIZE:] = jnp.ones((CHUNK, HEAD_SIZE), bf16)


def attention_kernel(q_ref, k_ref, v_ref, mask_ref, o_ref, keys, values, rows, maxima, total):
    chunk = pl.program_id(0)
    heads = q_ref.shape[2] // HEAD_SIZE

    @pl.when(chunk == 0)
    def _():
        build_keys(k_ref, v_ref, mask_ref, keys, values)

    square = (CHUNK, SEQ_BLOCKS)
    one_hot = iota(square, 0) // BLOCK_ROWS + chunk * (CHUNK // BLOCK_ROWS)
    one_hot = (one_hot == iota(square, 1)).astype(bf16)
    for h in range(heads):
        rows[h, :, 0:HEAD_SIZE] = q_ref[0, :, h * HEAD_SIZE : (h + 1) * HEAD_SIZE]
        rows[h, :, HEAD_SIZE:] = one_hot
    maxima[...] = jnp.full(maxima.shape, NEGATIVE, f32)
    total[...] = jnp.zeros(total.shape, f32)

    def tile(h, start, width, diagonal):
        scores = matmul(rows[h], keys[:, pl.ds(start, width)])
        if diagonal:
            shape = (CHUNK, width)
            scores = jnp.where(iota(shape, 1) <= iota(shape, 0), scores, NEGATIVE)
        old_max = maxima[h]
        new_max = jnp.maximum(old_max, jnp.max(scores, axis=1, keepdims=True))
        wide_max = jnp.concatenate([new_max] * (width // HEAD_SIZE), axis=1)
        weights = jnp.exp2((scores - wide_max) * LOG2_SCALE)
        factor = jnp.exp2((old_max - new_max) * LOG2_SCALE)
        maxima[h] = new_max
        added = matmul(weights.astype(bf16), values[pl.ds(start, width), :])
        total[h] = total[h] * jnp.concatenate([factor, factor], axis=1) + added

    def step(index, carry):
        for h in range(heads):
            tile(h, pl.multiple_of(index * KEY_TILE, KEY_TILE), KEY_TILE, False)
        return carry

    full = chunk * CHUNK // KEY_TILE
    lax.fori_loop(0, full, step, 0)

    @pl.when(chunk * CHUNK % KEY_TILE != 0)
    def _():
        for h in range(heads):
            tile(h, pl.multiple_of(full * KEY_TILE, CHUNK), CHUNK, False)

    for h in range(heads):
        tile(h, pl.multiple_of(chunk * CHUNK, CHUNK), CHUNK, True)
    for h in range(heads):
        summed = total[h]
        result = summed[:, 0:HEAD_SIZE] / summed[:, HEAD_SIZE:]
        o_ref[0, :, h * HEAD_SIZE : (h + 1) * HEAD_SIZE] = result.astype(bf16)


def attention(q, k, v, mask):
    chunks, _, width = q.shape
    heads = width // HEAD_SIZE
    tokens = k.shape[0]
    chunk_spec = pl.BlockSpec((1, CHUNK, width), lambda i: (i, 0, 0))
    key_spec = pl.BlockSpec((tokens, HEAD_SIZE), lambda i: (0, 0))
    return pl.pallas_call(
        attention_kernel,
        grid=(chunks,),
        in_specs=[
            chunk_spec,
            key_spec,
            key_spec,
            pl.BlockSpec((SEQ_BLOCKS, SEQ_BLOCKS), lambda i: (0, 0)),
        ],
        out_specs=chunk_spec,
        out_shape=jax.ShapeDtypeStruct(q.shape, bf16),
        scratch_shapes=[
            pltpu.VMEM((2 * HEAD_SIZE, tokens), bf16),
            pltpu.VMEM((tokens, 2 * HEAD_SIZE), bf16),
            pltpu.VMEM((heads, CHUNK, 2 * HEAD_SIZE), bf16),
            pltpu.VMEM((heads, CHUNK, HEAD_SIZE), f32),
            pltpu.VMEM((heads, CHUNK, 2 * HEAD_SIZE), f32),
        ],
        compiler_params=pltpu.CompilerParams(vmem_limit_bytes=40 * 2**20),
        cost_estimate=pl.CostEstimate(
            flops=40 * 10**9, bytes_accessed=12 * 2**20, transcendentals=36 * 2**20
        ),
    )(q, k, v, mask)


def swap_cores(x):
    count = lax.axis_size("seq")
    return lax.ppermute(x, "seq", [(i, i ^ 1) for i in range(count)])


def encode(tile_embeds, w_kv, core):
    tiles = tile_embeds.astype(f32)
    mean_square = jnp.mean(tiles * tiles, axis=-1, keepdims=True)
    normed = (tiles * lax.rsqrt(mean_square + EPS_NORM)).astype(bf16)
    half = w_kv.shape[1] // 2
    columns = lax.dynamic_slice_in_dim(w_kv, core * half, half, 1)
    columns = lax.all_gather(columns, "pool", axis=0, tiled=True)
    other = swap_cores(normed)
    mine = jnp.dot(normed, columns, preferred_element_type=f32).astype(bf16)
    theirs = jnp.dot(other, columns, preferred_element_type=f32).astype(bf16)
    arrived = swap_cores(theirs)
    return jnp.where(
        core == 0,
        jnp.concatenate([mine, arrived], axis=1),
        jnp.concatenate([arrived, mine], axis=1),
    )


def body(queries, text_kv, tile_embeds, stored_kv, w_kv, block_source, block_mask):
    pool_count = lax.axis_size("pool")
    seq_count = lax.axis_size("seq")
    my_pool = lax.axis_index("pool")
    my_seq = lax.axis_index("seq")
    core = my_seq % 2
    tokens = queries.shape[1]
    width = text_kv.shape[2]
    shard_blocks = tokens // BLOCK_ROWS
    store_slots = stored_kv.shape[1] // BLOCK_ROWS
    tile_slots = tile_embeds.shape[1] // BLOCK_ROWS
    entries = store_slots + tile_slots

    by_heads = queries[0].reshape(tokens, seq_count, -1).transpose(1, 0, 2)
    by_heads = lax.all_to_all(by_heads, "seq", split_axis=0, concat_axis=0, tiled=True)

    encoded = encode(tile_embeds[0], w_kv, core).reshape(tile_slots, BLOCK_ROWS, width)
    block_table = jnp.concatenate(
        [stored_kv[0].reshape(store_slots, BLOCK_ROWS, width), encoded], axis=0
    )

    is_image = block_source > 0
    source_index = jnp.maximum(block_source - 1, 0)
    source_pool = source_index // entries
    entry_index = source_index % entries
    outgoing = is_image & (source_pool == my_pool)
    order_rank = jnp.cumsum(outgoing.astype(jnp.int32), axis=1) - 1
    slot_ids = lax.iota(jnp.int32, SOURCE_CAP)
    selected = outgoing[:, None, :] & (order_rank[:, None, :] == slot_ids[None, :, None])
    picked_entry = jnp.sum(jnp.where(selected, entry_index[:, None, :], 0), axis=2)
    sending = jnp.take(block_table, picked_entry.reshape(-1), axis=0, mode="clip")
    sending = sending.reshape(-1, width)
    arrived = lax.all_to_all(sending, "pool", split_axis=0, concat_axis=0, tiled=True)
    arrived = arrived.reshape(pool_count * SOURCE_CAP, BLOCK_ROWS, width)

    my_codes = lax.dynamic_index_in_dim(block_source, my_pool, 0, keepdims=False)
    my_image = my_codes > 0
    my_source = jnp.maximum(my_codes - 1, 0) // entries
    block_order = lax.iota(jnp.int32, shard_blocks)
    same_source = (
        my_image[None, :]
        & (my_source[None, :] == my_source[:, None])
        & (block_order[None, :] < block_order[:, None])
    )
    my_rank = jnp.sum(same_source.astype(jnp.int32), axis=1)
    fetched = jnp.take(arrived, my_source * SOURCE_CAP + my_rank, axis=0, mode="clip")
    local_blocks = text_kv[0].reshape(shard_blocks, BLOCK_ROWS, width)
    assembled = jnp.where(my_image[:, None, None], fetched, local_blocks)

    parts = assembled.reshape(tokens, 2, seq_count // 2, HEAD_SIZE).transpose(2, 1, 0, 3)
    parts = parts.reshape(seq_count * tokens, HEAD_SIZE)
    half = lax.all_to_all(parts, "seq", split_axis=0, concat_axis=0, tiled=True)
    other = swap_cores(half)
    keys = jnp.where(core == 0, half, other)
    values = jnp.where(core == 0, other, half)

    attended = attention(by_heads, keys, values, block_mask[0])
    attended = lax.all_to_all(attended, "seq", split_axis=0, concat_axis=0, tiled=True)
    return attended.transpose(1, 0, 2).reshape(1, tokens, -1)


def solution(mesh):
    return jax.shard_map(
        body,
        mesh=mesh,
        in_specs=(
            P("pool", "seq", None),
            P("pool", "seq", None),
            P("seq", "pool", None),
            P("seq", "pool", None),
            P("pool", None),
            P(None, "seq"),
            P("pool", None, None),
        ),
        out_specs=P("pool", "seq", None),
        check_vma=False,
    )
```

```python
import functools
import jax
import jax.numpy as jnp
from jax import lax
from jax.experimental import pallas as pl
from jax.experimental.pallas import tpu as pltpu
from jax.sharding import PartitionSpec as P

HEAD_SIZE = 128
BLOCK_ROWS = 32
SOURCE_CAP = 2
CHUNK = 512
KEY_TILE = 1024
STEPS = ((1, 7), (3, 5), (2, 6), (4,), (0,))
SEQ_BLOCKS = 128
NEGATIVE = -1e30
EPS_NORM = 1e-06
LOG2_SCALE = HEAD_SIZE**-0.5 * 1.4426950408889634

bf16 = jnp.bfloat16
f32 = jnp.float32


def matmul(a, b):
    return lax.dot_general(a, b, (((1,), (0,)), ((), ())), preferred_element_type=f32)


def iota(shape, dim):
    return lax.broadcasted_iota(jnp.int32, shape, dim)


def build_keys(k_ref, v_ref, mask_ref, keys, values):
    square = (SEQ_BLOCKS, SEQ_BLOCKS)
    query_block, key_block = iota(square, 0), iota(square, 1)
    allowed = ((mask_ref[...] == 1) & (key_block < query_block)) | (key_block == query_block)
    bias = jnp.where(allowed, 0.0, NEGATIVE).astype(bf16)
    per_chunk = CHUNK // BLOCK_ROWS
    for t in range(k_ref.shape[0] // CHUNK):
        rows = slice(t * CHUNK, (t + 1) * CHUNK)
        spread = iota((SEQ_BLOCKS, CHUNK), 1) // BLOCK_ROWS + t * per_chunk
        spread = (spread == iota((SEQ_BLOCKS, CHUNK), 0)).astype(bf16)
        keys[0:HEAD_SIZE, rows] = k_ref[rows, :].T
        keys[HEAD_SIZE:, rows] = matmul(bias, spread).astype(bf16)
        values[rows, 0:HEAD_SIZE] = v_ref[rows, :]
        values[rows, HEAD_SIZE:] = jnp.ones((CHUNK, HEAD_SIZE), bf16)


def attention_kernel(chunk_ids, q_ref, k_ref, v_ref, mask_ref, *refs):
    o_refs = refs[:-5]
    count = len(o_refs)
    keys, values, rows, maxima, total = refs[-5:]
    position = pl.program_id(0)
    chunk = chunk_ids[position]
    heads = q_ref.shape[2] // HEAD_SIZE

    @pl.when(position == 0)
    def _():
        build_keys(k_ref, v_ref, mask_ref, keys, values)

    square = (CHUNK, SEQ_BLOCKS)
    one_hot = iota(square, 0) // BLOCK_ROWS + chunk * (CHUNK // BLOCK_ROWS)
    one_hot = (one_hot == iota(square, 1)).astype(bf16)
    for h in range(heads):
        rows[h, :, 0:HEAD_SIZE] = q_ref[0, :, h * HEAD_SIZE : (h + 1) * HEAD_SIZE]
        rows[h, :, HEAD_SIZE:] = one_hot
    maxima[...] = jnp.full(maxima.shape, NEGATIVE, f32)
    total[...] = jnp.zeros(total.shape, f32)

    def tile(h, start, width, diagonal):
        scores = matmul(rows[h], keys[:, pl.ds(start, width)])
        if diagonal:
            shape = (CHUNK, width)
            scores = jnp.where(iota(shape, 1) <= iota(shape, 0), scores, NEGATIVE)
        old_max = maxima[h]
        new_max = jnp.maximum(old_max, jnp.max(scores, axis=1, keepdims=True))
        wide_max = jnp.concatenate([new_max] * (width // HEAD_SIZE), axis=1)
        weights = jnp.exp2((scores - wide_max) * LOG2_SCALE)
        factor = jnp.exp2((old_max - new_max) * LOG2_SCALE)
        maxima[h] = new_max
        added = matmul(weights.astype(bf16), values[pl.ds(start, width), :])
        total[h] = total[h] * jnp.concatenate([factor, factor], axis=1) + added

    def step(index, carry):
        for h in range(heads):
            tile(h, pl.multiple_of(index * KEY_TILE, KEY_TILE), KEY_TILE, False)
        return carry

    full = chunk * CHUNK // KEY_TILE
    lax.fori_loop(0, full, step, 0)

    @pl.when(chunk * CHUNK % KEY_TILE != 0)
    def _():
        for h in range(heads):
            tile(h, pl.multiple_of(full * KEY_TILE, CHUNK), CHUNK, False)

    for h in range(heads):
        tile(h, pl.multiple_of(chunk * CHUNK, CHUNK), CHUNK, True)
    for i in range(count):

        @pl.when(position == i)
        def _():
            for h in range(heads):
                summed = total[h]
                result = summed[:, 0:HEAD_SIZE] / summed[:, HEAD_SIZE:]
                o_refs[i][:, h * HEAD_SIZE : (h + 1) * HEAD_SIZE] = result.astype(bf16)


def attention(chunk_ids, queries, k, v, mask):
    count = chunk_ids.shape[0]
    width = queries.shape[2]
    heads = width // HEAD_SIZE
    tokens = k.shape[0]
    chunk_spec = pl.BlockSpec((CHUNK, width), lambda i, ids: (0, 0))
    key_spec = pl.BlockSpec((tokens, HEAD_SIZE), lambda i, ids: (0, 0))
    return pl.pallas_call(
        attention_kernel,
        grid_spec=pltpu.PrefetchScalarGridSpec(
            num_scalar_prefetch=1,
            grid=(count,),
            in_specs=[pl.BlockSpec((1, CHUNK, width), lambda i, ids: (ids[i], 0, 0))]
            + [key_spec, key_spec, pl.BlockSpec((SEQ_BLOCKS, SEQ_BLOCKS), lambda i, ids: (0, 0))],
            out_specs=[chunk_spec] * count,
            scratch_shapes=[
                pltpu.VMEM((2 * HEAD_SIZE, tokens), bf16),
                pltpu.VMEM((tokens, 2 * HEAD_SIZE), bf16),
                pltpu.VMEM((heads, CHUNK, 2 * HEAD_SIZE), bf16),
                pltpu.VMEM((heads, CHUNK, HEAD_SIZE), f32),
                pltpu.VMEM((heads, CHUNK, 2 * HEAD_SIZE), f32),
            ],
        ),
        out_shape=[jax.ShapeDtypeStruct((CHUNK, width), bf16)] * count,
        compiler_params=pltpu.CompilerParams(vmem_limit_bytes=40 * 2**20),
        cost_estimate=pl.CostEstimate(
            flops=10**10 * count, bytes_accessed=3 * 2**20, transcendentals=5 * 2**20 * count
        ),
    )(chunk_ids, queries, k, v, mask)


def split_heads(x, count):
    rows, width = x.shape[0], x.shape[1] // count

    def copy(x_ref, o_ref):
        o_ref[0] = x_ref[...]

    return pl.pallas_call(
        copy,
        grid=(count,),
        in_specs=[pl.BlockSpec((rows, width), lambda i: (0, i))],
        out_specs=pl.BlockSpec((1, rows, width), lambda i: (i, 0, 0)),
        out_shape=jax.ShapeDtypeStruct((count, rows, width), x.dtype),
    )(x)


def join_columns(sources, parts, count, whole=None):
    rows, width = parts[0].shape
    each = len(parts)

    def copy(ids, *refs):
        for i in range(each):

            @pl.when(pl.program_id(0) == i)
            def _():
                refs[-1][...] = refs[i][...]

    operands = [sources, *parts] + ([] if whole is None else [whole])
    part_spec = pl.BlockSpec((rows, width), lambda i, ids: (0, 0))
    whole_spec = [] if whole is None else [pl.BlockSpec(memory_space=pl.ANY)]
    return pl.pallas_call(
        copy,
        grid_spec=pltpu.PrefetchScalarGridSpec(
            num_scalar_prefetch=1,
            grid=(each,),
            in_specs=[part_spec] * each + whole_spec,
            out_specs=pl.BlockSpec((rows, width), lambda i, ids: (0, ids[i])),
        ),
        out_shape=jax.ShapeDtypeStruct((rows, count * width), parts[0].dtype),
        input_output_aliases={} if whole is None else {len(operands) - 1: 0},
    )(*operands)


def swap_cores(x):
    count = lax.axis_size("seq")
    return lax.ppermute(x, "seq", [(i, i ^ 1) for i in range(count)])


def encode(tile_embeds, w_kv, core, beside):
    tiles = tile_embeds.astype(f32)
    mean_square = jnp.mean(tiles * tiles, axis=-1, keepdims=True)
    normed = (tiles * lax.rsqrt(mean_square + EPS_NORM)).astype(bf16)
    half = w_kv.shape[1] // 2
    columns = lax.dynamic_slice_in_dim(w_kv, core * half, half, 1)
    columns = lax.all_gather(columns, "pool", axis=0, tiled=True)
    other = swap_cores(normed)
    columns, beside = lax.optimization_barrier((columns, beside))
    mine = jnp.dot(normed, columns, preferred_element_type=f32).astype(bf16)
    theirs = jnp.dot(other, columns, preferred_element_type=f32).astype(bf16)
    arrived = swap_cores(theirs)
    encoded = jnp.where(
        core == 0,
        jnp.concatenate([mine, arrived], axis=1),
        jnp.concatenate([arrived, mine], axis=1),
    )
    return encoded, beside


def body(queries, text_kv, tile_embeds, stored_kv, w_kv, block_source, block_mask):
    pool_count = lax.axis_size("pool")
    seq_count = lax.axis_size("seq")
    my_pool = lax.axis_index("pool")
    my_seq = lax.axis_index("seq")
    core = my_seq % 2
    tokens = queries.shape[1]
    width = text_kv.shape[2]
    shard_blocks = tokens // BLOCK_ROWS
    store_slots = stored_kv.shape[1] // BLOCK_ROWS
    tile_slots = tile_embeds.shape[1] // BLOCK_ROWS
    entries = store_slots + tile_slots

    order = [step for part in STEPS for step in part]
    order_ids = jnp.array(order, jnp.int32)

    def to_next(x, steps):
        if steps == 0:
            return x
        return lax.ppermute(x, "seq", [(i, (i + steps) % seq_count) for i in range(seq_count)])

    by_heads = split_heads(queries[0], seq_count)
    by_heads = lax.all_to_all(by_heads, "seq", split_axis=0, concat_axis=0, tiled=True)

    encoded, by_heads = encode(tile_embeds[0], w_kv, core, by_heads)
    encoded = encoded.reshape(tile_slots, BLOCK_ROWS, width)
    block_table = jnp.concatenate(
        [stored_kv[0].reshape(store_slots, BLOCK_ROWS, width), encoded], axis=0
    )

    is_image = block_source > 0
    source_index = jnp.maximum(block_source - 1, 0)
    source_pool = source_index // entries
    entry_index = source_index % entries
    outgoing = is_image & (source_pool == my_pool)
    order_rank = jnp.cumsum(outgoing.astype(jnp.int32), axis=1) - 1
    slot_ids = lax.iota(jnp.int32, SOURCE_CAP)
    selected = outgoing[:, None, :] & (order_rank[:, None, :] == slot_ids[None, :, None])
    picked_entry = jnp.sum(jnp.where(selected, entry_index[:, None, :], 0), axis=2)
    sending = jnp.take(block_table, picked_entry.reshape(-1), axis=0, mode="clip")
    sending = sending.reshape(-1, width)
    arrived = lax.all_to_all(sending, "pool", split_axis=0, concat_axis=0, tiled=True)
    arrived = arrived.reshape(pool_count * SOURCE_CAP, BLOCK_ROWS, width)

    my_codes = lax.dynamic_index_in_dim(block_source, my_pool, 0, keepdims=False)
    my_image = my_codes > 0
    my_source = jnp.maximum(my_codes - 1, 0) // entries
    block_order = lax.iota(jnp.int32, shard_blocks)
    same_source = (
        my_image[None, :]
        & (my_source[None, :] == my_source[:, None])
        & (block_order[None, :] < block_order[:, None])
    )
    my_rank = jnp.sum(same_source.astype(jnp.int32), axis=1)
    fetched = jnp.take(arrived, my_source * SOURCE_CAP + my_rank, axis=0, mode="clip")
    local_blocks = text_kv[0].reshape(shard_blocks, BLOCK_ROWS, width)
    assembled = jnp.where(my_image[:, None, None], fetched, local_blocks)

    parts = assembled.reshape(tokens, 2, seq_count // 2, HEAD_SIZE).transpose(2, 1, 0, 3)
    parts = parts.reshape(seq_count * tokens, HEAD_SIZE)
    half = lax.all_to_all(parts, "seq", split_axis=0, concat_axis=0, tiled=True)
    other = swap_cores(half)
    keys = jnp.where(core == 0, half, other)
    values = jnp.where(core == 0, other, half)

    home, sent = [], []
    for part in STEPS:
        ids = (my_seq + jnp.array(part, jnp.int32)) % seq_count
        if len(sent) >= 2:
            ids, sent[-2] = lax.optimization_barrier((ids, sent[-2]))
        attended = attention(ids, by_heads, keys, values, block_mask[0])
        sent.append([to_next(x, step) for x, step in zip(attended, part)])
    home = [x for part in sent for x in part]
    sources = (my_seq - order_ids) % seq_count
    early = len(order) - 2
    whole = join_columns(sources[:early], home[:early], seq_count)
    whole = join_columns(sources[early:], home[early:], seq_count, whole)
    return whole[None]


def solution(mesh):
    return jax.shard_map(
        body,
        mesh=mesh,
        in_specs=(
            P("pool", "seq", None),
            P("pool", "seq", None),
            P("seq", "pool", None),
            P("seq", "pool", None),
            P("pool", None),
            P(None, "seq"),
            P("pool", None, None),
        ),
        out_specs=P("pool", "seq", None),
        check_vma=False,
    )
```

```python
import functools
import jax
import jax.numpy as jnp
from jax import lax
from jax.experimental import pallas as pl
from jax.experimental.pallas import tpu as pltpu
from jax.sharding import PartitionSpec as P

HEAD_SIZE = 128
BLOCK_ROWS = 32
SOURCE_CAP = 2
CHUNK = 512
KEY_TILE = 1024
ROWS = 256
STEPS = ((1, 7), (3, 5), (2, 6), (4,), (0,))
EARLY = 4
SEQ_BLOCKS = 128
NEGATIVE = -1e30
EPS_NORM = 1e-06
LOG2_SCALE = HEAD_SIZE**-0.5 * 1.4426950408889634

bf16 = jnp.bfloat16
f32 = jnp.float32


def matmul(a, b):
    return lax.dot_general(a, b, (((1,), (0,)), ((), ())), preferred_element_type=f32)


def iota(shape, dim):
    return lax.broadcasted_iota(jnp.int32, shape, dim)


def build_keys(start, own, other, core, allowed, keys, values):
    bias = jnp.where(allowed[...] == 1, 0.0, NEGATIVE).astype(bf16)
    rows = pl.ds(start, CHUNK)
    spread = (iota((SEQ_BLOCKS, CHUNK), 1) + start) // BLOCK_ROWS
    spread = (spread == iota((SEQ_BLOCKS, CHUNK), 0)).astype(bf16)
    mine, theirs = own[rows, :], other[rows, :]
    keys[0:HEAD_SIZE, rows] = jnp.where(core == 0, mine, theirs).T
    keys[HEAD_SIZE:, rows] = matmul(bias, spread).astype(bf16)
    values[rows, 0:HEAD_SIZE] = jnp.where(core == 0, theirs, mine)
    values[rows, HEAD_SIZE:] = jnp.ones((CHUNK, HEAD_SIZE), bf16)


def load_queries(q_ref, chunk, rows):
    shape = (CHUNK, SEQ_BLOCKS)
    one_hot = iota(shape, 0) // BLOCK_ROWS + chunk * (CHUNK // BLOCK_ROWS)
    one_hot = (one_hot == iota(shape, 1)).astype(bf16)
    for h in range(rows.shape[0]):
        rows[h, :, 0:HEAD_SIZE] = q_ref[:, h * HEAD_SIZE : (h + 1) * HEAD_SIZE]
        rows[h, :, HEAD_SIZE:] = one_hot


def attention_kernel(count, scalars, *refs):
    q_refs = refs[:count]
    own, other, allowed = refs[count : count + 3]
    o_refs = refs[count + 3 : 2 * count + 3]
    keys, values, rows, maxima, total, ahead, ahead_max = refs[2 * count + 3 :]
    position = pl.program_id(0)
    chunk, core = scalars[position], scalars[count]
    heads = rows.shape[0]

    @pl.when(position == 0)
    def _():
        for t in range(own.shape[0] // CHUNK):
            build_keys(t * CHUNK, own, other, core, allowed, keys, values)

    for i in range(count):

        @pl.when(position == i)
        def _():
            load_queries(q_refs[i], chunk, rows)

    maxima[...] = jnp.full(maxima.shape, NEGATIVE, f32)
    total[...] = jnp.zeros(total.shape, f32)
    groups = [(h, slice(r, r + ROWS)) for r in range(0, CHUNK, ROWS) for h in range(heads)]

    def scores_of(h, part, start, width):
        return matmul(rows[h, part], keys[:, pl.ds(start, width)])

    def lane_max(scores):
        largest = scores[:, 0:HEAD_SIZE]
        for i in range(HEAD_SIZE, scores.shape[1], HEAD_SIZE):
            largest = jnp.maximum(largest, scores[:, i : i + HEAD_SIZE])
        return largest

    def update(h, part, scores, largest, start):
        width = scores.shape[1]
        old_max = maxima[h, part]
        new_max = jnp.maximum(old_max, jnp.max(largest, axis=1, keepdims=True))
        wide_max = jnp.concatenate([new_max] * (width // HEAD_SIZE), axis=1)
        weights = jnp.exp2((scores - wide_max) * LOG2_SCALE)
        factor = jnp.exp2((old_max - new_max) * LOG2_SCALE)
        maxima[h, part] = new_max
        added = matmul(weights.astype(bf16), values[pl.ds(start, width), :])
        total[h, part] = total[h, part] * jnp.concatenate([factor, factor], axis=1) + added

    def prepare(index, start):
        scores = scores_of(*groups[index], start, KEY_TILE)
        ahead[index] = scores
        ahead_max[index] = lane_max(scores)

    full = chunk * CHUNK // KEY_TILE

    @pl.when(full > 0)
    def _():
        for index in range(len(groups)):
            prepare(index, 0)

        def step(tile, carry):
            start = pl.multiple_of(tile * KEY_TILE, KEY_TILE)
            for index, group in enumerate(groups):
                update(*group, ahead[index], ahead_max[index], start)
                prepare(index, pl.multiple_of(start + KEY_TILE, KEY_TILE))
            return carry

        lax.fori_loop(0, full - 1, step, 0)
        start = pl.multiple_of((full - 1) * KEY_TILE, KEY_TILE)
        for index, group in enumerate(groups):
            update(*group, ahead[index], ahead_max[index], start)

    def finish(before):
        start = pl.multiple_of(chunk * CHUNK - before, CHUNK)
        for h, part in groups:
            width = before + part.stop
            scores = scores_of(h, part, start, width)
            causal = iota((ROWS, ROWS), 1) <= iota((ROWS, ROWS), 0)
            last = jnp.where(causal, scores[:, width - ROWS :], NEGATIVE)
            if width > ROWS:
                last = jnp.concatenate([scores[:, : width - ROWS], last], axis=1)
            update(h, part, last, lane_max(last), start)

    for i in range(KEY_TILE // CHUNK):

        @pl.when(chunk % (KEY_TILE // CHUNK) == i)
        def _():
            finish(i * CHUNK)

    for i in range(count):

        @pl.when(position == i)
        def _():
            for h in range(heads):
                result = total[h, :, 0:HEAD_SIZE] / total[h, :, HEAD_SIZE:]
                o_refs[i][:, h * HEAD_SIZE : (h + 1) * HEAD_SIZE] = result.astype(bf16)


def attention(scalars, queries, own, other, allowed):
    count = len(queries)
    width = queries[0].shape[1]
    heads = width // HEAD_SIZE
    tokens = own.shape[0]
    groups = heads * CHUNK // ROWS

    def whole(shape):
        return pl.BlockSpec(shape, lambda i, ids: (0,) * len(shape))

    in_specs = [whole((CHUNK, width))] * count + [whole((tokens, HEAD_SIZE))] * 2
    in_specs.append(whole((SEQ_BLOCKS, SEQ_BLOCKS)))
    return pl.pallas_call(
        functools.partial(attention_kernel, count),
        grid_spec=pltpu.PrefetchScalarGridSpec(
            num_scalar_prefetch=1,
            grid=(count,),
            in_specs=in_specs,
            out_specs=[whole((CHUNK, width))] * count,
            scratch_shapes=[
                pltpu.VMEM((2 * HEAD_SIZE, tokens), bf16),
                pltpu.VMEM((tokens, 2 * HEAD_SIZE), bf16),
                pltpu.VMEM((heads, CHUNK, 2 * HEAD_SIZE), bf16),
                pltpu.VMEM((heads, CHUNK, HEAD_SIZE), f32),
                pltpu.VMEM((heads, CHUNK, 2 * HEAD_SIZE), f32),
                pltpu.VMEM((groups, ROWS, KEY_TILE), f32),
                pltpu.VMEM((groups, ROWS, HEAD_SIZE), f32),
            ],
        ),
        out_shape=[jax.ShapeDtypeStruct((CHUNK, width), bf16)] * count,
        compiler_params=pltpu.CompilerParams(vmem_limit_bytes=56 * 2**20),
        cost_estimate=pl.CostEstimate(
            flops=10**10 * count, bytes_accessed=4 * 2**20, transcendentals=5 * 2**20 * count
        ),
    )(scalars, *queries, own, other, allowed)


def split_columns(x, targets):
    count = targets.shape[0]
    rows, width = x.shape[0], x.shape[1] // count

    def copy(ids, x_ref, *refs):
        for i in range(count):

            @pl.when(pl.program_id(0) == i)
            def _():
                refs[i][...] = x_ref[...]

    return pl.pallas_call(
        copy,
        grid_spec=pltpu.PrefetchScalarGridSpec(
            num_scalar_prefetch=1,
            grid=(count,),
            in_specs=[pl.BlockSpec((rows, width), lambda i, ids: (0, ids[i]))],
            out_specs=[pl.BlockSpec((rows, width), lambda i, ids: (0, 0))] * count,
        ),
        out_shape=[jax.ShapeDtypeStruct((rows, width), x.dtype)] * count,
    )(targets, x)


def join_columns(sources, parts, count, whole=None):
    rows, width = parts[0].shape
    each = len(parts)

    def copy(ids, *refs):
        for i in range(each):

            @pl.when(pl.program_id(0) == i)
            def _():
                refs[-1][...] = refs[i][...]

    operands = [sources, *parts] + ([] if whole is None else [whole])
    part_spec = pl.BlockSpec((rows, width), lambda i, ids: (0, 0))
    whole_spec = [] if whole is None else [pl.BlockSpec(memory_space=pl.ANY)]
    return pl.pallas_call(
        copy,
        grid_spec=pltpu.PrefetchScalarGridSpec(
            num_scalar_prefetch=1,
            grid=(each,),
            in_specs=[part_spec] * each + whole_spec,
            out_specs=pl.BlockSpec((rows, width), lambda i, ids: (0, ids[i])),
        ),
        out_shape=jax.ShapeDtypeStruct((rows, count * width), parts[0].dtype),
        input_output_aliases={} if whole is None else {len(operands) - 1: 0},
    )(*operands)


def swap_cores(x):
    count = lax.axis_size("seq")
    return lax.ppermute(x, "seq", [(i, i ^ 1) for i in range(count)])


def encode(tile_embeds, w_kv, core, beside):
    half = w_kv.shape[1] // 2
    columns = lax.dynamic_slice_in_dim(w_kv, core * half, half, 1)
    columns = lax.all_gather(columns, "pool", axis=0, tiled=True)
    tiles = tile_embeds.astype(f32)
    mean_square = jnp.mean(tiles * tiles, axis=-1, keepdims=True)
    normed = (tiles * lax.rsqrt(mean_square + EPS_NORM)).astype(bf16)
    other = swap_cores(normed)
    first, second = jnp.where(core == 0, normed, other), jnp.where(core == 0, other, normed)
    both = jnp.concatenate([first, second])
    columns, beside = lax.optimization_barrier((columns, beside))
    return jnp.dot(both, columns, preferred_element_type=f32).astype(bf16), beside


def gather_seq(x, my_seq):
    count = lax.axis_size("seq")
    other = swap_cores(x)
    have = jnp.where(my_seq % 2 == 0, jnp.stack([x, other]), jnp.stack([other, x]))
    for steps in (2, 4):
        pairs = [(i, (i + steps) % count) for i in range(count)]
        have = jnp.concatenate([lax.ppermute(have, "seq", pairs), have])
    return jnp.roll(have, my_seq // 2 * 2 + 2, axis=0)


def earlier_same(flags, source):
    count = flags.shape[-1]
    earlier = lax.iota(jnp.int32, count)[None, :] < lax.iota(jnp.int32, count)[:, None]
    same = flags[..., None, :] & (source[..., None, :] == source[..., :, None]) & earlier
    return jnp.sum(same.astype(jnp.int32), axis=-1)


def pick(outgoing, entry):
    order_rank = jnp.cumsum(outgoing.astype(jnp.int32), axis=-1) - 1
    slot_ids = lax.iota(jnp.int32, SOURCE_CAP)
    selected = outgoing[..., None, :] & (order_rank[..., None, :] == slot_ids[:, None])
    return jnp.sum(jnp.where(selected, entry[..., None, :], 0), axis=-1)


def body(queries, text_kv, tile_embeds, stored_kv, w_kv, block_source, block_mask):
    pool_count = lax.axis_size("pool")
    seq_count = lax.axis_size("seq")
    my_pool = lax.axis_index("pool")
    my_seq = lax.axis_index("seq")
    core = my_seq % 2
    tokens = queries.shape[1]
    width = text_kv.shape[2]
    shard_blocks = tokens // BLOCK_ROWS
    store_slots = stored_kv.shape[1] // BLOCK_ROWS
    tile_slots = tile_embeds.shape[1] // BLOCK_ROWS
    entries = store_slots + tile_slots
    order = [step for part in STEPS for step in part]
    order_ids = jnp.array(order, jnp.int32)

    def to_next(x, steps):
        if steps == 0:
            return x
        return lax.ppermute(x, "seq", [(i, (i + steps) % seq_count) for i in range(seq_count)])

    pieces = split_columns(queries[0], (my_seq - order_ids) % seq_count)
    chunks = [to_next(piece, -step) for piece, step in zip(pieces, order)]

    def by_head(x, halves):
        x = x.reshape(x.shape[0], halves, seq_count // 2, HEAD_SIZE).transpose(2, 1, 0, 3)
        return x.reshape(-1, x.shape[2], HEAD_SIZE)

    local = jnp.concatenate([by_head(text_kv[0], 2), by_head(stored_kv[0], 2)], axis=1)
    local = lax.all_to_all(local, "seq", split_axis=0, concat_axis=0, tiled=True)

    codes = gather_seq(block_source, my_seq)
    is_image = codes > 0
    source_index = jnp.maximum(codes - 1, 0)
    source_pool, entry = source_index // entries, source_index % entries
    shard_ids = lax.iota(jnp.int32, seq_count)[:, None]
    picked = pick(is_image & (source_pool == my_pool), entry) + shard_ids[..., None] * entries
    picked = picked.transpose(1, 0, 2).reshape(-1)
    my_image = lax.dynamic_index_in_dim(is_image, my_pool, 1, keepdims=False)
    my_source = lax.dynamic_index_in_dim(source_pool, my_pool, 1, keepdims=False)
    place = (my_source * seq_count + shard_ids) * SOURCE_CAP + earlier_same(my_image, my_source)
    block_ids = lax.iota(jnp.int32, SEQ_BLOCKS)
    query_block, key_block = block_ids[:, None], block_ids[None, :]
    allowed = (block_mask[0] == 1) & (key_block < query_block) | (key_block == query_block)
    allowed = allowed.astype(jnp.int32)

    encoded, beside = encode(tile_embeds[0], w_kv, core, (local, chunks[:EARLY], picked, place))
    local, chunks[:EARLY], picked, place = beside
    groups = [list(range(c, seq_count, 2)) for c in range(2)]
    tiles = lax.all_to_all(
        by_head(encoded, 1), "seq", split_axis=0, concat_axis=0, axis_index_groups=groups, tiled=True
    )
    tiles = tiles.reshape(seq_count, tile_slots, BLOCK_ROWS, HEAD_SIZE)
    text, stored = local[:, :tokens], local[:, tokens:]
    stored = stored.reshape(seq_count, store_slots, BLOCK_ROWS, HEAD_SIZE)
    block_table = jnp.concatenate([stored, tiles], axis=1).reshape(-1, BLOCK_ROWS, HEAD_SIZE)
    sending = jnp.take(block_table, picked, axis=0, mode="clip").reshape(-1, HEAD_SIZE)
    arrived = lax.all_to_all(sending, "pool", split_axis=0, concat_axis=0, tiled=True)
    arrived, chunks[EARLY:] = lax.optimization_barrier((arrived, chunks[EARLY:]))
    fetched = jnp.take(
        arrived.reshape(-1, BLOCK_ROWS, HEAD_SIZE), place.reshape(-1), axis=0, mode="clip"
    )
    text = text.reshape(-1, BLOCK_ROWS, HEAD_SIZE)
    own = jnp.where(my_image.reshape(-1, 1, 1), fetched, text).reshape(-1, HEAD_SIZE)
    other = swap_cores(own)

    sent, done = [], 0
    for part in STEPS:
        ids = (my_seq + jnp.array(part, jnp.int32)) % seq_count
        if len(sent) >= 2:
            ids, sent[-2] = lax.optimization_barrier((ids, sent[-2]))
        scalars = jnp.concatenate([ids, core[None]])
        attended = attention(scalars, chunks[done : done + len(part)], own, other, allowed)
        sent.append([to_next(x, step) for x, step in zip(attended, part)])
        done += len(part)
    home = [x for part in sent for x in part]
    sources = (my_seq - order_ids) % seq_count
    early = len(order) - 2
    whole = join_columns(sources[:early], home[:early], seq_count)
    whole = join_columns(sources[early:], home[early:], seq_count, whole)
    return whole[None]


def solution(mesh):
    return jax.shard_map(
        body,
        mesh=mesh,
        in_specs=(
            P("pool", "seq", None),
            P("pool", "seq", None),
            P("seq", "pool", None),
            P("seq", "pool", None),
            P("pool", None),
            P(None, "seq"),
            P("pool", None, None),
        ),
        out_specs=P("pool", "seq", None),
        check_vma=False,
    )
```

```python
import functools
import jax
import jax.numpy as jnp
from jax import lax
from jax.experimental import pallas as pl
from jax.experimental.pallas import tpu as pltpu
from jax.sharding import PartitionSpec as P

HEAD_SIZE = 128
BLOCK_ROWS = 32
SOURCE_CAP = 2
CHUNK = 512
KEY_TILE = 1024
ROWS = 256
STEPS = ((1, 7), (3, 5), (2, 6), (4,), (0,))
EARLY = 4
SEQ_BLOCKS = 128
NEGATIVE = -1e30
EPS_NORM = 1e-06
LOG2_SCALE = HEAD_SIZE**-0.5 * 1.4426950408889634

bf16 = jnp.bfloat16
f32 = jnp.float32


def matmul(a, b):
    return lax.dot_general(a, b, (((1,), (0,)), ((), ())), preferred_element_type=f32)


def iota(shape, dim):
    return lax.broadcasted_iota(jnp.int32, shape, dim)


def build_keys(start, own, other, core, allowed, keys, values):
    bias = jnp.where(allowed[...] == 1, 0.0, NEGATIVE).astype(bf16)
    rows = pl.ds(start, CHUNK)
    spread = (iota((SEQ_BLOCKS, CHUNK), 1) + start) // BLOCK_ROWS
    spread = (spread == iota((SEQ_BLOCKS, CHUNK), 0)).astype(bf16)
    mine, theirs = own[rows, :], other[rows, :]
    keys[0:HEAD_SIZE, rows] = jnp.where(core == 0, mine, theirs).T
    keys[HEAD_SIZE:, rows] = matmul(bias, spread).astype(bf16)
    values[rows, 0:HEAD_SIZE] = jnp.where(core == 0, theirs, mine)
    values[rows, HEAD_SIZE:] = jnp.ones((CHUNK, HEAD_SIZE), bf16)


def load_queries(q_ref, chunk, rows):
    shape = (CHUNK, SEQ_BLOCKS)
    one_hot = iota(shape, 0) // BLOCK_ROWS + chunk * (CHUNK // BLOCK_ROWS)
    one_hot = (one_hot == iota(shape, 1)).astype(bf16)
    for h in range(rows.shape[0]):
        rows[h, :, 0:HEAD_SIZE] = q_ref[:, h * HEAD_SIZE : (h + 1) * HEAD_SIZE]
        rows[h, :, HEAD_SIZE:] = one_hot


def attention_kernel(count, scalars, *refs):
    q_refs = refs[:count]
    own, other, allowed = refs[count : count + 3]
    o_refs = refs[count + 3 : 2 * count + 3]
    keys, values, rows, maxima, total, ahead, ahead_max = refs[2 * count + 3 :]
    position = pl.program_id(0)
    chunk, core = scalars[position], scalars[count]
    heads = rows.shape[0]

    @pl.when(position == 0)
    def _():
        for t in range(own.shape[0] // CHUNK):
            build_keys(t * CHUNK, own, other, core, allowed, keys, values)

    for i in range(count):

        @pl.when(position == i)
        def _():
            load_queries(q_refs[i], chunk, rows)

    maxima[...] = jnp.full(maxima.shape, NEGATIVE, f32)
    total[...] = jnp.zeros(total.shape, f32)
    groups = [(h, slice(r, r + ROWS)) for r in range(0, CHUNK, ROWS) for h in range(heads)]

    def scores_of(h, part, start, width):
        return matmul(rows[h, part], keys[:, pl.ds(start, width)])

    def lane_max(scores):
        largest = scores[:, 0:HEAD_SIZE]
        for i in range(HEAD_SIZE, scores.shape[1], HEAD_SIZE):
            largest = jnp.maximum(largest, scores[:, i : i + HEAD_SIZE])
        return largest

    def update(h, part, scores, largest, start):
        width = scores.shape[1]
        old_max = maxima[h, part]
        new_max = jnp.maximum(old_max, jnp.max(largest, axis=1, keepdims=True))
        wide_max = jnp.concatenate([new_max] * (width // HEAD_SIZE), axis=1)
        weights = jnp.exp2((scores - wide_max) * LOG2_SCALE)
        factor = jnp.exp2((old_max - new_max) * LOG2_SCALE)
        maxima[h, part] = new_max
        added = matmul(weights.astype(bf16), values[pl.ds(start, width), :])
        total[h, part] = total[h, part] * jnp.concatenate([factor, factor], axis=1) + added

    def prepare(index, start):
        scores = scores_of(*groups[index], start, KEY_TILE)
        ahead[index] = scores
        ahead_max[index] = lane_max(scores)

    full = chunk * CHUNK // KEY_TILE

    @pl.when(full > 0)
    def _():
        for index in range(len(groups)):
            prepare(index, 0)

        def step(tile, carry):
            start = pl.multiple_of(tile * KEY_TILE, KEY_TILE)
            for index, group in enumerate(groups):
                update(*group, ahead[index], ahead_max[index], start)
                prepare(index, pl.multiple_of(start + KEY_TILE, KEY_TILE))
            return carry

        lax.fori_loop(0, full - 1, step, 0)
        start = pl.multiple_of((full - 1) * KEY_TILE, KEY_TILE)
        for index, group in enumerate(groups):
            update(*group, ahead[index], ahead_max[index], start)

    def finish(before):
        start = pl.multiple_of(chunk * CHUNK - before, CHUNK)
        for h, part in groups:
            width = before + part.stop
            scores = scores_of(h, part, start, width)
            causal = iota((ROWS, ROWS), 1) <= iota((ROWS, ROWS), 0)
            last = jnp.where(causal, scores[:, width - ROWS :], NEGATIVE)
            if width > ROWS:
                last = jnp.concatenate([scores[:, : width - ROWS], last], axis=1)
            update(h, part, last, lane_max(last), start)

    for i in range(KEY_TILE // CHUNK):

        @pl.when(chunk % (KEY_TILE // CHUNK) == i)
        def _():
            finish(i * CHUNK)

    for i in range(count):

        @pl.when(position == i)
        def _():
            for h in range(heads):
                result = total[h, :, 0:HEAD_SIZE] / total[h, :, HEAD_SIZE:]
                o_refs[i][:, h * HEAD_SIZE : (h + 1) * HEAD_SIZE] = result.astype(bf16)


def attention(scalars, queries, own, other, allowed):
    count = len(queries)
    width = queries[0].shape[1]
    heads = width // HEAD_SIZE
    tokens = own.shape[0]
    groups = heads * CHUNK // ROWS

    def whole(shape):
        return pl.BlockSpec(shape, lambda i, ids: (0,) * len(shape))

    in_specs = [whole((CHUNK, width))] * count + [whole((tokens, HEAD_SIZE))] * 2
    in_specs.append(whole((SEQ_BLOCKS, SEQ_BLOCKS)))
    return pl.pallas_call(
        functools.partial(attention_kernel, count),
        grid_spec=pltpu.PrefetchScalarGridSpec(
            num_scalar_prefetch=1,
            grid=(count,),
            in_specs=in_specs,
            out_specs=[whole((CHUNK, width))] * count,
            scratch_shapes=[
                pltpu.VMEM((2 * HEAD_SIZE, tokens), bf16),
                pltpu.VMEM((tokens, 2 * HEAD_SIZE), bf16),
                pltpu.VMEM((heads, CHUNK, 2 * HEAD_SIZE), bf16),
                pltpu.VMEM((heads, CHUNK, HEAD_SIZE), f32),
                pltpu.VMEM((heads, CHUNK, 2 * HEAD_SIZE), f32),
                pltpu.VMEM((groups, ROWS, KEY_TILE), f32),
                pltpu.VMEM((groups, ROWS, HEAD_SIZE), f32),
            ],
        ),
        out_shape=[jax.ShapeDtypeStruct((CHUNK, width), bf16)] * count,
        compiler_params=pltpu.CompilerParams(vmem_limit_bytes=36 * 2**20),
        cost_estimate=pl.CostEstimate(
            flops=10**10 * count, bytes_accessed=4 * 2**20, transcendentals=5 * 2**20 * count
        ),
    )(scalars, *queries, own, other, allowed)


def split_columns(x, targets):
    count = targets.shape[0]
    rows, width = x.shape[0], x.shape[1] // count

    def copy(ids, x_ref, *refs):
        for i in range(count):

            @pl.when(pl.program_id(0) == i)
            def _():
                refs[i][...] = x_ref[...]

    return pl.pallas_call(
        copy,
        grid_spec=pltpu.PrefetchScalarGridSpec(
            num_scalar_prefetch=1,
            grid=(count,),
            in_specs=[pl.BlockSpec((rows, width), lambda i, ids: (0, ids[i]))],
            out_specs=[pl.BlockSpec((rows, width), lambda i, ids: (0, 0))] * count,
        ),
        out_shape=[jax.ShapeDtypeStruct((rows, width), x.dtype)] * count,
    )(targets, x)


def join_columns(sources, parts, count, whole=None):
    rows, width = parts[0].shape
    each = len(parts)

    def copy(ids, *refs):
        for i in range(each):

            @pl.when(pl.program_id(0) == i)
            def _():
                refs[-1][...] = refs[i][...]

    operands = [sources, *parts] + ([] if whole is None else [whole])
    part_spec = pl.BlockSpec((rows, width), lambda i, ids: (0, 0))
    whole_spec = [] if whole is None else [pl.BlockSpec(memory_space=pl.ANY)]
    return pl.pallas_call(
        copy,
        grid_spec=pltpu.PrefetchScalarGridSpec(
            num_scalar_prefetch=1,
            grid=(each,),
            in_specs=[part_spec] * each + whole_spec,
            out_specs=pl.BlockSpec((rows, width), lambda i, ids: (0, ids[i])),
        ),
        out_shape=jax.ShapeDtypeStruct((rows, count * width), parts[0].dtype),
        input_output_aliases={} if whole is None else {len(operands) - 1: 0},
    )(*operands)


def swap_cores(x):
    count = lax.axis_size("seq")
    return lax.ppermute(x, "seq", [(i, i ^ 1) for i in range(count)])


def encode(tile_embeds, w_kv, core, beside):
    half = w_kv.shape[1] // 2
    columns = lax.dynamic_slice_in_dim(w_kv, core * half, half, 1)
    columns = lax.all_gather(columns, "pool", axis=0, tiled=True)
    tiles = tile_embeds.astype(f32)
    mean_square = jnp.mean(tiles * tiles, axis=-1, keepdims=True)
    normed = (tiles * lax.rsqrt(mean_square + EPS_NORM)).astype(bf16)
    other = swap_cores(normed)
    first, second = jnp.where(core == 0, normed, other), jnp.where(core == 0, other, normed)
    both = jnp.concatenate([first, second])
    columns, beside = lax.optimization_barrier((columns, beside))
    return jnp.dot(both, columns, preferred_element_type=f32).astype(bf16), beside


def gather_seq(x, my_seq):
    count = lax.axis_size("seq")
    other = swap_cores(x)
    have = jnp.where(my_seq % 2 == 0, jnp.stack([x, other]), jnp.stack([other, x]))
    for steps in (2, 4):
        pairs = [(i, (i + steps) % count) for i in range(count)]
        have = jnp.concatenate([lax.ppermute(have, "seq", pairs), have])
    return jnp.roll(have, my_seq // 2 * 2 + 2, axis=0)


def earlier_same(flags, source):
    count = flags.shape[-1]
    earlier = lax.iota(jnp.int32, count)[None, :] < lax.iota(jnp.int32, count)[:, None]
    same = flags[..., None, :] & (source[..., None, :] == source[..., :, None]) & earlier
    return jnp.sum(same.astype(jnp.int32), axis=-1)


def pick(outgoing, entry):
    order_rank = jnp.cumsum(outgoing.astype(jnp.int32), axis=-1) - 1
    slot_ids = lax.iota(jnp.int32, SOURCE_CAP)
    selected = outgoing[..., None, :] & (order_rank[..., None, :] == slot_ids[:, None])
    return jnp.sum(jnp.where(selected, entry[..., None, :], 0), axis=-1)


def body(queries, text_kv, tile_embeds, stored_kv, w_kv, block_source, block_mask):
    pool_count = lax.axis_size("pool")
    seq_count = lax.axis_size("seq")
    my_pool = lax.axis_index("pool")
    my_seq = lax.axis_index("seq")
    core = my_seq % 2
    tokens = queries.shape[1]
    width = text_kv.shape[2]
    shard_blocks = tokens // BLOCK_ROWS
    store_slots = stored_kv.shape[1] // BLOCK_ROWS
    tile_slots = tile_embeds.shape[1] // BLOCK_ROWS
    entries = store_slots + tile_slots
    order = [step for part in STEPS for step in part]
    order_ids = jnp.array(order, jnp.int32)

    def to_next(x, steps):
        if steps == 0:
            return x
        return lax.ppermute(x, "seq", [(i, (i + steps) % seq_count) for i in range(seq_count)])

    pieces = split_columns(queries[0], (my_seq - order_ids) % seq_count)
    chunks = [to_next(piece, -step) for piece, step in zip(pieces, order)]

    def by_head(x, halves):
        x = x.reshape(x.shape[0], halves, seq_count // 2, HEAD_SIZE).transpose(2, 1, 0, 3)
        return x.reshape(-1, x.shape[2], HEAD_SIZE)

    local = jnp.concatenate([by_head(text_kv[0], 2), by_head(stored_kv[0], 2)], axis=1)
    local = lax.all_to_all(local, "seq", split_axis=0, concat_axis=0, tiled=True)

    codes = gather_seq(block_source, my_seq)
    is_image = codes > 0
    source_index = jnp.maximum(codes - 1, 0)
    source_pool, entry = source_index // entries, source_index % entries
    shard_ids = lax.iota(jnp.int32, seq_count)[:, None]
    picked = pick(is_image & (source_pool == my_pool), entry) + shard_ids[..., None] * entries
    picked = picked.transpose(1, 0, 2).reshape(-1)
    my_image = lax.dynamic_index_in_dim(is_image, my_pool, 1, keepdims=False)
    my_source = lax.dynamic_index_in_dim(source_pool, my_pool, 1, keepdims=False)
    place = (my_source * seq_count + shard_ids) * SOURCE_CAP + earlier_same(my_image, my_source)
    block_ids = lax.iota(jnp.int32, SEQ_BLOCKS)
    query_block, key_block = block_ids[:, None], block_ids[None, :]
    allowed = (block_mask[0] == 1) & (key_block < query_block) | (key_block == query_block)
    allowed = allowed.astype(jnp.int32)

    encoded, beside = encode(tile_embeds[0], w_kv, core, (local, chunks[:EARLY], picked, place))
    local, chunks[:EARLY], picked, place = beside
    groups = [list(range(c, seq_count, 2)) for c in range(2)]
    tiles = lax.all_to_all(
        by_head(encoded, 1), "seq", split_axis=0, concat_axis=0, axis_index_groups=groups, tiled=True
    )
    tiles = tiles.reshape(seq_count, tile_slots, BLOCK_ROWS, HEAD_SIZE)
    text, stored = local[:, :tokens], local[:, tokens:]
    stored = stored.reshape(seq_count, store_slots, BLOCK_ROWS, HEAD_SIZE)
    block_table = jnp.concatenate([stored, tiles], axis=1).reshape(-1, BLOCK_ROWS, HEAD_SIZE)
    sending = jnp.take(block_table, picked, axis=0, mode="clip").reshape(-1, HEAD_SIZE)
    arrived = lax.all_to_all(sending, "pool", split_axis=0, concat_axis=0, tiled=True)
    arrived, chunks[EARLY:] = lax.optimization_barrier((arrived, chunks[EARLY:]))
    fetched = jnp.take(
        arrived.reshape(-1, BLOCK_ROWS, HEAD_SIZE), place.reshape(-1), axis=0, mode="clip"
    )
    text = text.reshape(-1, BLOCK_ROWS, HEAD_SIZE)
    own = jnp.where(my_image.reshape(-1, 1, 1), fetched, text).reshape(-1, HEAD_SIZE)
    other = swap_cores(own)

    sent, done = [], 0
    for part in STEPS:
        ids = (my_seq + jnp.array(part, jnp.int32)) % seq_count
        if len(sent) >= 2:
            ids, sent[-2] = lax.optimization_barrier((ids, sent[-2]))
        scalars = jnp.concatenate([ids, core[None]])
        attended = attention(scalars, chunks[done : done + len(part)], own, other, allowed)
        sent.append([to_next(x, step) for x, step in zip(attended, part)])
        done += len(part)
    home = [x for part in sent for x in part]
    sources = (my_seq - order_ids) % seq_count
    early = len(order) - 2
    whole = join_columns(sources[:early], home[:early], seq_count)
    whole = join_columns(sources[early:], home[early:], seq_count, whole)
    return whole[None]


def solution(mesh):
    return jax.shard_map(
        body,
        mesh=mesh,
        in_specs=(
            P("pool", "seq", None),
            P("pool", "seq", None),
            P("seq", "pool", None),
            P("seq", "pool", None),
            P("pool", None),
            P(None, "seq"),
            P("pool", None, None),
        ),
        out_specs=P("pool", "seq", None),
        check_vma=False,
    )
```
